512 devices in a mesh: zone: 32 (over z, x_hi), freq: 16 (over x_lo, y, core).
Axes of the slice: x: 4 (x_hi: 2, x_lo: 2; x = x_hi * 2 + x_lo), y: 4, z: 16, core: 2. Of those that a mesh axis runs over, the one named last changes fastest.
Arguments:
- modulus: float32 [256, 3, 1, 1024], P('zone'), may hold values from 0.3 to 1.5
- first_moment: float32 [256, 3, 1, 1024], P('zone'), may hold values from -6 to 6
- second_moment: float32 [256, 3, 1, 1024], P('zone'), may hold values from 0.5 to 4
- fiber: float32 [256, 1, 1024], P('zone'), may hold values from -1 to 1
- measured: float32 [16, 128, 2, 8, 1024], P('freq', 'zone'), may hold values from -6 to 6
- wave_sq: float32 [16], P('freq'), may hold values from 0.5 to 5
- send_list: int32 [32, 32, 2], P('zone'), may hold values from -1 to 7, as said below
- brick_list: int32 [128, 8], P('zone'), may hold values from 0 to 63, as said below
Outputs:
- new_modulus: float32 [256, 3, 1, 1024], P('zone')
- new_first: float32 [256, 3, 1, 1024], P('zone')
- new_second: float32 [256, 3, 1, 1024], P('zone')
The draws below stay inside these ranges and needn't reach their ends.
Inputs may be any that keep to these rules, and one draw needn't show every extreme that they name: `send_list`: entries are -1 or distinct local brick indices; for each owner and zone group the live slots are c < some count of 0 to 2, and owner o sends 2 bricks to group (o + 1) % 32. `brick_list`: every entry names a live slot of its zone group.
All inputs are finite; a program needn't handle non-finite values.
Results may differ from the reference program's by a relative error of at most 0.0001.
Values sent between devices are 32-bit elements; how exact they have to be, the bound alone decides.
A program may use at most 64 MiB of HBM per device.

```python
import math
import jax
import jax.numpy as jnp
from jax import lax

NB_DEV = 8
SZ_DEV = 4
BX = 1
BY = 32
BZ = 32
K = 8
CAP = 2
SWEEPS = 6
ZGROUPS = 32
FREQS = 16
BRICKS = 256
SUBZONES = 128


def route_tables(key):
    base = jax.random.fold_in(key, 4242)
    key_count = jax.random.fold_in(base, 1)
    key_perm = jax.random.fold_in(base, 2)
    key_pick = jax.random.fold_in(base, 3)
    key_shuffle = jax.random.fold_in(base, 5)
    counts = jax.random.randint(key_count, (ZGROUPS, ZGROUPS), 0, CAP + 1)
    owner_idx = jnp.arange(ZGROUPS, dtype=jnp.int32)[:, None]
    dest_idx = jnp.arange(ZGROUPS, dtype=jnp.int32)[None, :]
    counts = jnp.where(dest_idx == (owner_idx + 1) % ZGROUPS, CAP, counts)
    counts = jnp.where((owner_idx == 0) & (dest_idx == 0), CAP, counts).astype(jnp.int32)
    perm_keys = jax.random.split(key_perm, ZGROUPS * ZGROUPS)
    chosen = jax.vmap(lambda one_key: jax.random.permutation(one_key, NB_DEV)[:CAP])(perm_keys)
    chosen = chosen.reshape(ZGROUPS, ZGROUPS, CAP).astype(jnp.int32)
    chosen = chosen.at[0, 1 % ZGROUPS, 0].set(NB_DEV - 1)
    chosen = chosen.at[0, 1 % ZGROUPS, 1].set(0)
    slot_idx = jnp.arange(CAP, dtype=jnp.int32)[None, None, :]
    live_mask = slot_idx < counts[:, :, None]
    send_table = jnp.where(live_mask, chosen, -1).astype(jnp.int32)
    live_dest = jnp.transpose(live_mask, (1, 0, 2)).reshape(ZGROUPS, ZGROUPS * CAP)
    ordering = jnp.argsort(jnp.where(live_dest, 0, 1).astype(jnp.int32), axis=-1, stable=True).astype(jnp.int32)
    live_total = jnp.sum(live_dest.astype(jnp.int32), axis=-1).astype(jnp.int32)
    entries = SZ_DEV * K
    picks = jax.random.randint(key_pick, (ZGROUPS, entries), 0, live_total[:, None]).astype(jnp.int32)
    seq_idx = jnp.arange(entries, dtype=jnp.int32)[None, :]
    positions = jnp.where(seq_idx < live_total[:, None], seq_idx, picks).astype(jnp.int32)
    shuffle_keys = jax.random.split(key_shuffle, ZGROUPS)
    shuffles = jax.vmap(lambda one_key: jax.random.permutation(one_key, entries))(shuffle_keys).astype(jnp.int32)
    positions = jnp.take_along_axis(positions, shuffles, axis=-1)
    brick_table = jnp.take_along_axis(ordering, positions, axis=-1)
    brick_table = brick_table.reshape(ZGROUPS * SZ_DEV, K).astype(jnp.int32)
    top_slot = (ZGROUPS - 1) * CAP + CAP - 1
    brick_table = brick_table.at[0, 0].set(top_slot)
    brick_table = brick_table.at[0, 1].set(0)
    return (send_table, brick_table.astype(jnp.int32))


def draw_send_list(key, part):
    return route_tables(key)[0]


def draw_brick_list(key, part):
    return route_tables(key)[1]


def shard_levels(own_key, shape, cuts, least, largest):
    loudness, own = 1.0, jax.random.fold_in(own_key, 6)
    for position, blocks in cuts:
        draws = jnp.exp(jax.random.uniform(jax.random.fold_in(own, position), (blocks,), jnp.float32, least / len(cuts), largest / len(cuts)))
        loudness = loudness * jnp.repeat(draws, shape[position] // blocks).reshape([-1 if axis == position else 1 for axis in range(len(shape))])
    return loudness


def gaussian(key, extent, width, reach, cuts=(), held_as=jnp.bfloat16):
    level = shard_levels(key, extent, cuts, -0.22, 0.18) if cuts else 1.0
    values = jax.random.normal(key, extent, jnp.float32) * width * level
    return jnp.minimum(jnp.maximum(values, -reach), reach).astype(held_as)


def setup_inputs(seed: int = 0) -> dict:
    streams_of = jax.random.split(jax.random.key(seed), 9)
    return {
        "modulus": jnp.clip(0.3 + 1.2 * jax.random.uniform(streams_of[0], (BRICKS, 3, BX, BY * BZ), jnp.float32) ** shard_levels(streams_of[0], (BRICKS, 3, BX, BY * BZ), ((0, 32),), -0.2, 0.2), 0.3, 1.5),
        "first_moment": gaussian(streams_of[1], (BRICKS, 3, BX, BY * BZ), 1.0, 6.0, ((0, 32),), jnp.float32),
        "second_moment": jnp.clip(jnp.exp(math.log(4.0) - 2.0794415 * jax.random.uniform(streams_of[2], (BRICKS, 3, BX, BY * BZ), jnp.float32) ** shard_levels(streams_of[2], (BRICKS, 3, BX, BY * BZ), ((0, 32),), -0.2, 0.2)), 0.5, 4.0),
        "fiber": jnp.clip(jax.random.uniform(streams_of[3], (BRICKS, BX, BY * BZ), jnp.float32, -1.0, 1.0) * shard_levels(streams_of[3], (BRICKS, BX, BY * BZ), ((0, 32),), -0.4, 0.0), -1.0, 1.0),
        "measured": gaussian(streams_of[4], (FREQS, SUBZONES, 2, K * BX, BY * BZ), 1.0, 6.0, ((0, 16), (1, 32)), jnp.float32),
        "wave_sq": jnp.clip(jnp.exp(math.log(5.0) - 2.3025851 * jax.random.uniform(streams_of[5], (FREQS,), jnp.float32) ** shard_levels(streams_of[5], (FREQS,), ((0, 16),), -0.2, 0.2)), 0.5, 5.0),
        "send_list": draw_send_list(jax.random.fold_in(streams_of[8], 71), 0),
        "brick_list": draw_brick_list(jax.random.fold_in(streams_of[8], 71), 0),
    }


relax_rate = 0.25
learn_rate = 0.1
beta_first = 0.9
beta_second = 0.99
smooth_rate = 0.5
adam_eps = 1e-08

def beside_sum(cube):
    padded = jnp.pad(cube, ((0, 0), (1, 1), (1, 1), (1, 1)))
    total = padded[:, 2:, 1:-1, 1:-1] + padded[:, :-2, 1:-1, 1:-1]
    total = total + padded[:, 1:-1, 2:, 1:-1] + padded[:, 1:-1, :-2, 1:-1]
    return total + padded[:, 1:-1, 1:-1, 2:] + padded[:, 1:-1, 1:-1, :-2]

def misfit(moduli, fiber_tile, observed, wave_value):
    shear = (moduli[0] + (moduli[1] - moduli[0]) * fiber_tile * fiber_tile).reshape(-1, BY, BZ)
    damping = moduli[2].reshape(-1, BY, BZ)
    diagonal_term = 6.0 * shear + wave_value
    start_field = observed.reshape(2, -1, BY, BZ)
    field = start_field
    for sweep_index in range(SWEEPS):
        stencil = 6.0 * field - beside_sum(field)
        resid_real = shear * (stencil[0] - damping * stencil[1]) - wave_value * field[0]
        resid_imag = shear * (stencil[1] + damping * stencil[0]) - wave_value * field[1]
        field = field - relax_rate * jnp.stack([resid_real, resid_imag]) / diagonal_term
    gap = field - start_field
    return jnp.sum(gap * gap)

def update(moduli, first_moment, second_moment, fiber_tile, descent):
    new_first = beta_first * first_moment + (1.0 - beta_first) * descent
    new_second = beta_second * second_moment + (1.0 - beta_second) * descent * descent
    stepped = moduli - learn_rate * new_first / (jnp.sqrt(new_second) + adam_eps)
    shaped = stepped.reshape(stepped.shape[:-1] + (-1, BZ))
    lower_cell = jnp.concatenate([shaped[..., :1], shaped[..., :-1]], axis=-1).reshape(stepped.shape)
    upper_cell = jnp.concatenate([shaped[..., 1:], shaped[..., -1:]], axis=-1).reshape(stepped.shape)
    weight = smooth_rate * (fiber_tile * fiber_tile)[:, None]
    smoothed = stepped + weight * (0.5 * (lower_cell + upper_cell) - stepped)
    return (smoothed, new_first, new_second)

def reference(modulus, first_moment, second_moment, fiber, measured, wave_sq, send_list, brick_list):
    rows_brick = modulus.shape[2]
    depth = modulus.shape[3]
    owner_ids = (brick_list // CAP).astype(jnp.int32)
    slot_ids = (brick_list % CAP).astype(jnp.int32)
    dest_ids = (jnp.arange(SUBZONES, dtype=jnp.int32) // SZ_DEV)[:, None]
    local_ids = send_list[owner_ids, dest_ids, slot_ids]
    global_ids = (owner_ids * NB_DEV + local_ids).astype(jnp.int32)
    stacked = jnp.concatenate([modulus, fiber[:, None]], axis=1)

    def per_freq(grad_total, freq_item):
        observed_all, wave_value = freq_item

        def solve(subzone_item):
            brick_ids, observed = subzone_item
            picked_rows = stacked[brick_ids]
            subzone_par = jnp.swapaxes(picked_rows, 0, 1).reshape(4, K * rows_brick, depth)
            gradient = jax.grad(misfit)(subzone_par[:3], subzone_par[3], observed, wave_value)
            return jnp.swapaxes(gradient.reshape(3, K, rows_brick, depth), 0, 1)
        gradients = lax.map(solve, (global_ids, observed_all))
        grad_total = grad_total.at[global_ids.reshape(-1)].add(gradients.reshape(-1, 3, rows_brick, depth))
        return (grad_total, None)
    start_total = jnp.zeros((BRICKS, 3, rows_brick, depth), jnp.float32)
    grad_total, unused = lax.scan(per_freq, start_total, (measured, wave_sq))
    intersection = jnp.zeros((BRICKS,), jnp.float32).at[global_ids.reshape(-1)].add(1.0)
    descent = grad_total / (FREQS * jnp.maximum(intersection, 1.0))[:, None, None, None]
    return update(modulus, first_moment, second_moment, fiber, descent)
```

```python
import functools

import jax
import jax.numpy as jnp
from jax import lax
from jax.experimental import pallas as pl
from jax.experimental.pallas import tpu as pltpu
from jax.sharding import PartitionSpec as P

BZ = 32
K = 8
NB = 8
SUBZ = 4
CAP = 2
YH = 8
LANES = 128
SWEEPS = 6
GROUP = 4

relax_rate = 0.25
learn_rate = 0.1
beta_first = 0.9
beta_second = 0.99
smooth_rate = 0.5
adam_eps = 1e-08

MESH = pl.DeviceIdType.MESH
HIGHEST = lax.Precision.HIGHEST


def beside_sum(x):
    lane = lax.broadcasted_iota(jnp.int32, x.shape, 3)
    sub = lax.broadcasted_iota(jnp.int32, x.shape, 2)
    z = lane % BZ
    none = jnp.zeros_like(x[:, :1])
    up = pltpu.roll(x, BZ, 3)
    up = jnp.where(lane < BZ, jnp.concatenate([none, up[:, :-1]], 1), up)
    down = pltpu.roll(x, LANES - BZ, 3)
    down = jnp.where(lane >= LANES - BZ, jnp.concatenate([down[:, 1:], none], 1), down)
    total = up + down
    total += jnp.where(z > 0, pltpu.roll(x, 1, 3), 0.0)
    total += jnp.where(z < BZ - 1, pltpu.roll(x, LANES - 1, 3), 0.0)
    total += jnp.where(sub > 0, pltpu.roll(x, 1, 2), 0.0)
    return total + jnp.where(sub < K - 1, pltpu.roll(x, K - 1, 2), 0.0)


def exchange(
    zones,
    freqs,
    group,
    mod_hbm,
    fib_hbm,
    meas_hbm,
    wave_ref,
    send_ref,
    brick_ref,
    out_ref,
    mod_v,
    fib_v,
    val_v,
    out1,
    in1,
    cnt_out,
    cnt_in,
    ent,
    in2,
    meas_v,
    wave_v,
    sten0,
    hist_v,
    hist_w,
    gsum,
    gout,
    in3,
    out4,
    in4,
    own5,
    in5,
    local_sem,
    send_sem,
    recv_sem,
):
    subs = SUBZ // group
    slots = zones * CAP
    me_z = lax.axis_index("zone")
    me_f = lax.axis_index("freq")
    plane = lax.rem(me_f, 2)
    row = lax.div(me_f, 2)
    member = lax.rem(me_f, group)
    base = me_f - member

    load_mod = pltpu.make_async_copy(mod_hbm, mod_v, local_sem.at[0])
    load_fib = pltpu.make_async_copy(fib_hbm, fib_v, local_sem.at[1])
    load_meas = pltpu.make_async_copy(
        meas_hbm.at[pl.ds(member * subs, subs)], meas_v.at[member], local_sem.at[2]
    )
    load_mod.start()
    load_fib.start()
    load_meas.start()

    barrier = pltpu.get_barrier_semaphore()

    def greet_z(i, c):
        pl.semaphore_signal(
            barrier, inc=1, device_id=(lax.rem(me_z + i, zones), me_f), device_id_type=MESH
        )
        return c

    def greet_f(i, c):
        pl.semaphore_signal(
            barrier, inc=1, device_id=(me_z, lax.rem(me_f + i, freqs)), device_id_type=MESH
        )
        return c

    lax.fori_loop(1, zones, greet_z, 0)
    lax.fori_loop(1, freqs, greet_f, 0)

    load_mod.wait()
    load_fib.wait()
    first = mod_v[pl.ds(row, NB, stride=3 * YH), :]
    second = mod_v[pl.ds(YH + row, NB, stride=3 * YH), :]
    damp = mod_v[pl.ds(2 * YH + row, NB, stride=3 * YH), :]
    fibre = fib_v[pl.ds(row, NB, stride=YH), :]
    shear = first + (second - first) * fibre * fibre
    val_v[...] = jnp.where(plane == 0, shear, damp)
    for d in range(zones):
        for c in range(CAP):
            pick = jnp.maximum(send_ref[0, c, d], 0)
            out1[d * CAP + c : d * CAP + c + 1, :] = val_v[pl.ds(pick, 1), :]

    pl.semaphore_wait(barrier, zones + freqs - 2)

    def over_z(src, dst, n):
        def body(i, c):
            peer = lax.rem(me_z + i, zones)
            pltpu.make_async_remote_copy(
                src_ref=src(peer),
                dst_ref=dst,
                send_sem=send_sem.at[n],
                recv_sem=recv_sem.at[n],
                device_id=(peer, me_f),
                device_id_type=MESH,
            ).start()
            return c

        lax.fori_loop(1, zones, body, 0)

    def over_f(src, dst, n):
        def body(i, c):
            peer = lax.rem(me_f + i, freqs)
            pltpu.make_async_remote_copy(
                src_ref=src(peer),
                dst_ref=dst,
                send_sem=send_sem.at[n],
                recv_sem=recv_sem.at[n],
                device_id=(me_z, peer),
                device_id_type=MESH,
            ).start()
            return c

        lax.fori_loop(1, freqs, body, 0)

    def arrived(ref, n):
        pltpu.make_async_copy(ref, ref, recv_sem.at[n]).wait()

    def sent(ref, n):
        pltpu.make_async_copy(ref, ref, send_sem.at[n]).wait()

    mine2 = pl.ds(me_z * CAP, CAP)
    over_z(lambda p: out1.at[pl.ds(p * CAP, CAP)], in1.at[mine2], 0)
    in1[mine2, :] = out1[mine2, :]

    wave_v[member] = jnp.full((8, LANES), wave_ref[0], jnp.float32)

    def share(i, c):
        j = lax.rem(member + i, group)
        pltpu.make_async_remote_copy(
            src_ref=meas_hbm.at[pl.ds(j * subs, subs)],
            dst_ref=meas_v.at[member],
            send_sem=send_sem.at[1],
            recv_sem=recv_sem.at[1],
            device_id=(me_z, base + j),
            device_id_type=MESH,
        ).start()
        pltpu.make_async_remote_copy(
            src_ref=wave_v.at[member],
            dst_ref=wave_v.at[member],
            send_sem=send_sem.at[2],
            recv_sem=recv_sem.at[2],
            device_id=(me_z, base + j),
            device_id_type=MESH,
        ).start()
        return c

    if group > 1:
        lax.fori_loop(1, group, share, 0)

    entries = SUBZ * K
    lane_e = lax.broadcasted_iota(jnp.int32, (1, entries), 1)
    names = jnp.zeros((1, entries), jnp.int32)
    for e in range(entries):
        names = jnp.where(lane_e == e, brick_ref[e // K, e % K], names)
    named = (lax.broadcasted_iota(jnp.int32, (slots, entries), 0) == names).astype(jnp.float32)
    cnt_out[...] = jnp.broadcast_to(jnp.sum(named, 1, keepdims=True), (slots, LANES))
    over_z(lambda p: cnt_out.at[pl.ds(p * CAP, CAP)], cnt_in.at[mine2], 3)
    cnt_in[mine2, :] = cnt_out[mine2, :]

    arrived(in1.at[pl.ds(0, (zones - 1) * CAP)], 0)
    for e in range(entries):
        ent[e // K, e % K : e % K + 1, :] = in1[pl.ds(brick_ref[e // K, e % K], 1), :]
    over_f(
        lambda p: ent.at[pl.ds(lax.rem(p, group) * subs, subs)],
        in2.at[me_f],
        4,
    )
    in2[me_f] = ent[pl.ds(member * subs, subs)]

    load_meas.wait()
    if group > 1:
        arrived(meas_v.at[pl.ds(0, group - 1)], 1)
        arrived(wave_v.at[pl.ds(0, group - 1)], 2)

    def first_stencil(i, c):
        g, s = lax.div(i, subs), lax.rem(i, subs)
        sten0[i] = beside_sum(meas_v[g, s])
        return c

    lax.fori_loop(0, group * subs, first_stencil, 0)

    lane_s = lax.broadcasted_iota(jnp.int32, (1, slots), 1)
    held = jnp.zeros((1, slots), jnp.int32)
    for d in range(zones):
        for c in range(CAP):
            held = jnp.where(lane_s == d * CAP + c, send_ref[0, c, d], held)
    holds = (lax.broadcasted_iota(jnp.int32, (NB, slots), 0) == held).astype(jnp.float32)

    arrived(in2.at[pl.ds(0, freqs - 1)], 4)

    gsum[...] = jnp.zeros_like(gsum)

    def solve(i, c):
        g, s = lax.div(i, subs), lax.rem(i, subs)
        wave = wave_v[g][None]
        shear = jnp.stack([in2[2 * y, s] for y in range(YH)])
        damp = jnp.stack([in2[2 * y + 1, s] for y in range(YH)])
        inv = 1.0 / (6.0 * shear + wave)
        a = relax_rate * shear * inv
        b = a * damp
        start = meas_v[g, s]
        field = start
        near = sten0[i]
        for t in range(SWEEPS):
            if t:
                near = beside_sum(field)
            six = 6.0 * field
            w = near - six
            v = w - six
            hist_v[t] = v
            hist_w[t] = w
            real = 1.25 * field[0] + a * v[0] - b * w[1]
            imag = 1.25 * field[1] + a * v[1] + b * w[0]
            field = jnp.stack([real, imag])
        lam = 2.0 * (field - start)
        grad_a = jnp.zeros_like(a)
        grad_b = jnp.zeros_like(a)
        for t in reversed(range(SWEEPS)):
            v = hist_v[t]
            w = hist_w[t]
            grad_a += lam[0] * v[0] + lam[1] * v[1]
            grad_b += lam[1] * w[0] - lam[0] * w[1]
            if t:
                a_lam = a * lam
                push = a_lam + jnp.stack([b * lam[1], -(b * lam[0])])
                lam = 1.25 * lam - 6.0 * (push + a_lam) + beside_sum(push)
        gsum[s, 0] += (grad_a + damp * grad_b) * (relax_rate * wave * inv * inv)
        gsum[s, 1] += a * grad_b
        return c

    lax.fori_loop(0, group * subs, solve, 0)

    for s in range(subs):
        for p in range(2):
            for y in range(YH):
                gout[2 * y + p, s] = gsum[s, p, y]
    over_f(lambda p: gout.at[p], in3.at[me_f], 5)
    in3[me_f] = gout[me_f]
    arrived(in3.at[pl.ds(0, freqs - 1)], 5)
    parts = []
    for j in range(group):
        total = in3[j]
        for m in range(1, freqs // group):
            total = total + in3[m * group + j]
        parts.append(total.reshape(subs * K, LANES))
    grads = jnp.concatenate(parts, 0)
    out4[...] = jnp.dot(named, grads, precision=HIGHEST, preferred_element_type=jnp.float32)
    over_z(lambda p: out4.at[pl.ds(p * CAP, CAP)], in4.at[mine2], 6)
    in4[mine2, :] = out4[mine2, :]
    arrived(cnt_in.at[pl.ds(0, (zones - 1) * CAP)], 3)
    uses = jnp.dot(holds, cnt_in[...], precision=HIGHEST, preferred_element_type=jnp.float32)
    scale = 1.0 / (freqs * jnp.maximum(uses, 1.0))
    arrived(in4.at[pl.ds(0, (zones - 1) * CAP)], 6)
    owned = jnp.dot(holds, in4[...], precision=HIGHEST, preferred_element_type=jnp.float32)
    own5[...] = owned * scale
    mine8 = pl.ds(pl.multiple_of(me_f * NB, NB), NB)
    over_f(lambda p: own5, in5.at[mine8], 7)
    in5[mine8, :] = own5[...]
    arrived(in5.at[pl.ds(0, (freqs - 1) * NB)], 7)
    out_ref[...] = in5[...]

    sent(out1.at[pl.ds(0, (zones - 1) * CAP)], 0)
    if group > 1:
        sent(meas_v.at[pl.ds(0, group - 1)], 1)
        sent(wave_v.at[pl.ds(0, group - 1)], 2)
    sent(cnt_out.at[pl.ds(0, (zones - 1) * CAP)], 3)
    sent(in2.at[pl.ds(0, freqs - 1)], 4)
    sent(gout.at[pl.ds(0, freqs - 1)], 5)
    sent(out4.at[pl.ds(0, (zones - 1) * CAP)], 6)
    sent(in5.at[pl.ds(0, (freqs - 1) * NB)], 7)


def update(desc_ref, mod_ref, first_ref, second_ref, fib_ref, new_mod, new_first, new_second):
    lane = lax.broadcasted_iota(jnp.int32, (YH, LANES), 1)
    z = lane % BZ
    for b in range(NB):
        fibre = fib_ref[b * YH : (b + 1) * YH, :]
        square = fibre * fibre
        by_shear = desc_ref[pl.ds(b, YH, stride=2 * NB), :]
        by_damp = desc_ref[pl.ds(NB + b, YH, stride=2 * NB), :]
        by_second = by_shear * square
        for j, descent in enumerate((by_shear - by_second, by_second, by_damp)):
            at = slice((b * 3 + j) * YH, (b * 3 + j + 1) * YH)
            m1 = beta_first * first_ref[at, :] + (1.0 - beta_first) * descent
            m2 = beta_second * second_ref[at, :] + (1.0 - beta_second) * descent * descent
            stepped = mod_ref[at, :] - learn_rate * m1 / (jnp.sqrt(m2) + adam_eps)
            lower = jnp.where(z > 0, pltpu.roll(stepped, 1, 1), stepped)
            upper = jnp.where(z < BZ - 1, pltpu.roll(stepped, LANES - 1, 1), stepped)
            new_first[at, :] = m1
            new_second[at, :] = m2
            new_mod[at, :] = stepped + smooth_rate * square * (0.5 * (lower + upper) - stepped)


def on_device(
    zones, freqs, modulus, first_moment, second_moment, fiber, measured, wave_sq, send_list, brick_list
):
    group = GROUP
    subs = SUBZ // group
    slots = zones * CAP
    mod = modulus.reshape(NB * 3 * YH, LANES)
    m1 = first_moment.reshape(NB * 3 * YH, LANES)
    m2 = second_moment.reshape(NB * 3 * YH, LANES)
    fib = fiber.reshape(NB * YH, LANES)
    meas = measured.reshape(SUBZ, 2, K, YH, LANES).transpose(0, 1, 3, 2, 4)
    f32 = jnp.float32
    vmem = pltpu.VMEM
    any_spec = pl.BlockSpec(memory_space=pl.ANY)
    smem_spec = pl.BlockSpec(memory_space=pltpu.SMEM)
    vmem_spec = pl.BlockSpec(memory_space=vmem)
    plane_shape = (2, YH, K, LANES)
    descent = pl.pallas_call(
        functools.partial(exchange, zones, freqs, group),
        out_shape=jax.ShapeDtypeStruct((freqs * NB, LANES), f32),
        in_specs=[any_spec, any_spec, any_spec, smem_spec, smem_spec, smem_spec],
        out_specs=vmem_spec,
        scratch_shapes=[
            vmem((NB * 3 * YH, LANES), f32),
            vmem((NB * YH, LANES), f32),
            vmem((NB, LANES), f32),
            vmem((slots, LANES), f32),
            vmem((slots, LANES), f32),
            vmem((slots, LANES), f32),
            vmem((slots, LANES), f32),
            vmem((SUBZ, K, LANES), f32),
            vmem((freqs, subs, K, LANES), f32),
            vmem((group, subs) + plane_shape, f32),
            vmem((group, 8, LANES), f32),
            vmem((group * subs,) + plane_shape, f32),
            vmem((SWEEPS,) + plane_shape, f32),
            vmem((SWEEPS,) + plane_shape, f32),
            vmem((subs,) + plane_shape, f32),
            vmem((freqs, subs, K, LANES), f32),
            vmem((freqs, subs, K, LANES), f32),
            vmem((slots, LANES), f32),
            vmem((slots, LANES), f32),
            vmem((NB, LANES), f32),
            vmem((freqs * NB, LANES), f32),
            pltpu.SemaphoreType.DMA((3,)),
            pltpu.SemaphoreType.DMA((8,)),
            pltpu.SemaphoreType.DMA((8,)),
        ],
        compiler_params=pltpu.CompilerParams(
            collective_id=0, has_side_effects=True, vmem_limit_bytes=60 * 2**20
        ),
    )(mod, fib, meas, wave_sq, send_list.transpose(0, 2, 1), brick_list)
    made = jax.ShapeDtypeStruct((NB * 3 * YH, LANES), f32)
    outs = pl.pallas_call(
        update,
        out_shape=(made, made, made),
        in_specs=[vmem_spec] * 5,
        out_specs=(vmem_spec,) * 3,
    )(descent, mod, m1, m2, fib)
    return tuple(o.reshape(modulus.shape) for o in outs)


def solution(mesh):
    placed = (
        P("zone", None, None, None),
        P("zone", None, None, None),
        P("zone", None, None, None),
        P("zone", None, None),
        P("freq", "zone", None, None, None),
        P("freq"),
        P("zone", None, None),
        P("zone", None),
    )
    return jax.shard_map(
        functools.partial(on_device, mesh.shape["zone"], mesh.shape["freq"]),
        mesh=mesh,
        in_specs=placed,
        out_specs=(P("zone", None, None, None),) * 3,
        check_vma=False,
    )
```

```python
import functools

import jax
import jax.numpy as jnp
from jax import lax
from jax.experimental import pallas as pl
from jax.experimental.pallas import tpu as pltpu
from jax.sharding import PartitionSpec as P

BZ = 32
K = 8
NB = 8
SUBZ = 4
CAP = 2
YH = 8
LANES = 128
SWEEPS = 6
BY = 32
STEP = 8
GROUP = 4

relax_rate = 0.25
learn_rate = 0.1
beta_first = 0.9
beta_second = 0.99
smooth_rate = 0.5
adam_eps = 1e-08

MESH = pl.DeviceIdType.MESH
HIGHEST = lax.Precision.HIGHEST


def quarters(shape=(K, LANES)):
    lane = lax.broadcasted_iota(jnp.int32, shape, len(shape) - 1)
    return lane < 2 * BZ, lane % (2 * BZ) < BZ


def turn(x, n):
    return pltpu.roll(x, n * BZ, 1)


def transposed(x):
    low, even = quarters()
    n0 = jnp.where(low, x[0], turn(x[2], 2))
    n1 = jnp.where(low, x[1], turn(x[3], 2))
    n2 = jnp.where(low, turn(x[0], 2), x[2])
    n3 = jnp.where(low, turn(x[1], 2), x[3])
    return (
        jnp.where(even, n0, turn(n1, 1)),
        jnp.where(even, turn(n0, 3), n1),
        jnp.where(even, n2, turn(n3, 1)),
        jnp.where(even, turn(n2, 3), n3),
    )


def spread(x):
    low, even = quarters()
    r = (x, turn(x, 1), turn(x, 2), turn(x, 3))
    return tuple(
        jnp.where(
            low,
            jnp.where(even, r[(-q) % 4], r[(1 - q) % 4]),
            jnp.where(even, r[(2 - q) % 4], r[(3 - q) % 4]),
        )
        for q in range(4)
    )


def folded(x):
    low, even = quarters()
    p0 = jnp.where(low, x[0], x[2]) + turn(jnp.where(low, x[2], x[0]), 2)
    p1 = jnp.where(low, x[1], x[3]) + turn(jnp.where(low, x[3], x[1]), 2)
    rest = jnp.where(even, p1, p0)
    return jnp.where(even, p0, p1) + jnp.where(even, turn(rest, 3), turn(rest, 1))


def beside_sum(ref, y):
    x = ref[:, y + 1 : y + 1 + STEP]
    lane = lax.broadcasted_iota(jnp.int32, x.shape, 3)
    sub = lax.broadcasted_iota(jnp.int32, x.shape, 2)
    z = lane % BZ
    total = ref[:, y : y + STEP] + ref[:, y + 2 : y + 2 + STEP]
    total += jnp.where(z > 0, pltpu.roll(x, 1, 3), 0.0)
    total += jnp.where(z < BZ - 1, pltpu.roll(x, LANES - 1, 3), 0.0)
    total += jnp.where(sub > 0, pltpu.roll(x, 1, 2), 0.0)
    return x, total + jnp.where(sub < K - 1, pltpu.roll(x, K - 1, 2), 0.0)


def exchange(
    zones,
    freqs,
    group,
    mod_hbm,
    fib_hbm,
    meas_hbm,
    wave_ref,
    send_ref,
    brick_ref,
    out_ref,
    mod_v,
    fib_v,
    val_v,
    out1,
    in1,
    cnt_out,
    cnt_in,
    ent,
    in2,
    meas_v,
    wave_v,
    field_v,
    sten_v,
    a_v,
    b_v,
    damp_v,
    slope_v,
    lam_v,
    push_v,
    by_a_v,
    by_b_v,
    gout,
    in3,
    out4,
    in4,
    own5,
    in5,
    local_sem,
    send_sem,
    recv_sem,
):
    subs = SUBZ // group
    slots = zones * CAP
    me_z = lax.axis_index("zone")
    me_f = lax.axis_index("freq")
    plane = lax.rem(me_f, 2)
    row = lax.div(me_f, 2)
    member = lax.rem(me_f, group)
    base = me_f - member

    load_mod = pltpu.make_async_copy(mod_hbm, mod_v, local_sem.at[0])
    load_fib = pltpu.make_async_copy(fib_hbm, fib_v, local_sem.at[1])
    load_meas = pltpu.make_async_copy(
        meas_hbm.at[pl.ds(member * subs, subs)], meas_v.at[member], local_sem.at[2]
    )
    barrier = pltpu.get_barrier_semaphore()

    def greet_z(i, c):
        pl.semaphore_signal(
            barrier, inc=1, device_id=(lax.rem(me_z + zones + zones // 2 + jnp.where(lax.rem(i, 2) == 0, lax.div(i, 2), -lax.div(i, 2)), zones), me_f), device_id_type=MESH
        )
        return c

    def greet_f(i, c):
        pl.semaphore_signal(
            barrier, inc=1, device_id=(me_z, lax.rem(me_f + i, freqs)), device_id_type=MESH
        )
        return c

    lax.fori_loop(1, zones, greet_z, 0)
    lax.fori_loop(1, freqs, greet_f, 0)
    load_mod.start()
    load_fib.start()
    load_meas.start()

    load_mod.wait()
    load_fib.wait()
    first = mod_v[pl.ds(row, NB, stride=3 * YH), :]
    second = mod_v[pl.ds(YH + row, NB, stride=3 * YH), :]
    damp = mod_v[pl.ds(2 * YH + row, NB, stride=3 * YH), :]
    fibre = fib_v[pl.ds(row, NB, stride=YH), :]
    shear = first + (second - first) * fibre * fibre
    val_v[...] = jnp.where(plane == 0, shear, damp)
    for d in range(zones):
        for c in range(CAP):
            pick = jnp.maximum(send_ref[0, c, d], 0)
            out1[d * CAP + c : d * CAP + c + 1, :] = val_v[pl.ds(pick, 1), :]

    pl.semaphore_wait(barrier, zones + freqs - 2)

    def over_z(src, dst, n):
        def body(i, c):
            k = lax.div(i, 2)
            peer = lax.rem(me_z + zones + zones // 2 + jnp.where(lax.rem(i, 2) == 0, k, -k), zones)
            pltpu.make_async_remote_copy(
                src_ref=src(peer),
                dst_ref=dst,
                send_sem=send_sem.at[n],
                recv_sem=recv_sem.at[n],
                device_id=(peer, me_f),
                device_id_type=MESH,
            ).start()
            return c

        lax.fori_loop(1, zones, body, 0)

    def over_f(src, dst, n):
        def body(i, c):
            peer = lax.rem(me_f + i, freqs)
            pltpu.make_async_remote_copy(
                src_ref=src(peer),
                dst_ref=dst,
                send_sem=send_sem.at[n],
                recv_sem=recv_sem.at[n],
                device_id=(me_z, peer),
                device_id_type=MESH,
            ).start()
            return c

        lax.fori_loop(1, freqs, body, 0)

    def arrived(ref, n):
        pltpu.make_async_copy(ref, ref, recv_sem.at[n]).wait()

    def sent(ref, n):
        pltpu.make_async_copy(ref, ref, send_sem.at[n]).wait()

    mine2 = pl.ds(me_z * CAP, CAP)
    over_z(lambda p: out1.at[pl.ds(p * CAP, CAP)], in1.at[mine2], 0)
    in1[mine2, :] = out1[mine2, :]

    wave_v[member] = jnp.full((8, LANES), wave_ref[0], jnp.float32)

    def share(i, c):
        j = lax.rem(member + i, group)
        pltpu.make_async_remote_copy(
            src_ref=meas_hbm.at[pl.ds(j * subs, subs)],
            dst_ref=meas_v.at[member],
            send_sem=send_sem.at[1],
            recv_sem=recv_sem.at[1],
            device_id=(me_z, base + j),
            device_id_type=MESH,
        ).start()
        pltpu.make_async_remote_copy(
            src_ref=wave_v.at[member],
            dst_ref=wave_v.at[member],
            send_sem=send_sem.at[2],
            recv_sem=recv_sem.at[2],
            device_id=(me_z, base + j),
            device_id_type=MESH,
        ).start()
        return c

    if group > 1:
        lax.fori_loop(1, group, share, 0)

    entries = SUBZ * K
    lane_e = lax.broadcasted_iota(jnp.int32, (1, entries), 1)
    names = jnp.zeros((1, entries), jnp.int32)
    for e in range(entries):
        names = jnp.where(lane_e == e, brick_ref[e // K, e % K], names)
    named = (lax.broadcasted_iota(jnp.int32, (slots, entries), 0) == names).astype(jnp.float32)
    cnt_out[...] = jnp.broadcast_to(jnp.sum(named, 1, keepdims=True), (slots, LANES))
    over_z(lambda p: cnt_out.at[pl.ds(p * CAP, CAP)], cnt_in.at[mine2], 3)
    cnt_in[mine2, :] = cnt_out[mine2, :]

    arrived(in1.at[pl.ds(0, (zones - 1) * CAP)], 0)
    for e in range(entries):
        ent[e // K, e % K : e % K + 1, :] = in1[pl.ds(brick_ref[e // K, e % K], 1), :]
    over_f(
        lambda p: ent.at[pl.ds(lax.rem(p, group) * subs, subs)],
        in2.at[me_f],
        4,
    )
    in2[me_f] = ent[pl.ds(member * subs, subs)]

    load_meas.wait()
    if group > 1:
        arrived(meas_v.at[pl.ds(0, group - 1)], 1)
        arrived(wave_v.at[pl.ds(0, group - 1)], 2)

    for t in range(SWEEPS):
        field_v[t, :, 0] = jnp.zeros((2, K, LANES), jnp.float32)
        field_v[t, :, BY + 1] = jnp.zeros((2, K, LANES), jnp.float32)
    push_v[:, 0] = jnp.zeros((2, K, LANES), jnp.float32)
    push_v[:, BY + 1] = jnp.zeros((2, K, LANES), jnp.float32)
    for p in range(2):
        for y in range(YH):
            for q, tile in enumerate(transposed([meas_v[g, 0, p, y] for g in range(group)])):
                field_v[0, p, 1 + 4 * y + q] = tile
    low, even = quarters()
    wave = jnp.where(
        low,
        jnp.where(even, wave_v[0], wave_v[1]),
        jnp.where(even, wave_v[2], wave_v[3]),
    )
    for y in range(0, BY, STEP):
        x, near = beside_sum(field_v.at[0], y)
        sten_v[0, :, y : y + STEP] = near - 6.0 * x

    lane_s = lax.broadcasted_iota(jnp.int32, (1, slots), 1)
    held = jnp.zeros((1, slots), jnp.int32)
    for d in range(zones):
        for c in range(CAP):
            held = jnp.where(lane_s == d * CAP + c, send_ref[0, c, d], held)
    holds = (lax.broadcasted_iota(jnp.int32, (NB, slots), 0) == held).astype(jnp.float32)

    arrived(in2.at[pl.ds(0, freqs - 1)], 4)

    for y in range(YH):
        for q, (shear, damp) in enumerate(zip(spread(in2[2 * y, 0]), spread(in2[2 * y + 1, 0]))):
            inv = 1.0 / (6.0 * shear + wave)
            a = relax_rate * shear * inv
            a_v[4 * y + q] = a
            b_v[4 * y + q] = a * damp
            damp_v[4 * y + q] = damp
            slope_v[4 * y + q] = relax_rate * wave * inv * inv

    for t in range(SWEEPS):
        for y in range(0, BY, STEP):
            rows = slice(y, y + STEP)
            if t:
                x, near = beside_sum(field_v.at[t], y)
                six = 6.0 * x
                w = near - six
                sten_v[t, :, rows] = w
            else:
                x = field_v[0, :, y + 1 : y + 1 + STEP]
                six = 6.0 * x
                w = sten_v[0, :, rows]
            v = w - six
            a, b = a_v[rows], b_v[rows]
            real = 1.25 * x[0] + (a * v[0] - b * w[1])
            imag = 1.25 * x[1] + (a * v[1] + b * w[0])
            if t < SWEEPS - 1:
                field_v[t + 1, 0, y + 1 : y + 1 + STEP] = real
                field_v[t + 1, 1, y + 1 : y + 1 + STEP] = imag
            else:
                lam_v[0, rows] = 2.0 * (real - field_v[0, 0, y + 1 : y + 1 + STEP])
                lam_v[1, rows] = 2.0 * (imag - field_v[0, 1, y + 1 : y + 1 + STEP])
    for t in reversed(range(SWEEPS)):
        for y in range(0, BY, STEP):
            rows = slice(y, y + STEP)
            lam = lam_v[:, rows]
            w = sten_v[t, :, rows]
            v = w - 6.0 * field_v[t, :, y + 1 : y + 1 + STEP]
            by_a = lam[0] * v[0] + lam[1] * v[1]
            by_b = lam[1] * w[0] - lam[0] * w[1]
            if t < SWEEPS - 1:
                by_a += by_a_v[rows]
                by_b += by_b_v[rows]
            a, b = a_v[rows], b_v[rows]
            if t:
                by_a_v[rows] = by_a
                by_b_v[rows] = by_b
                push_v[0, y + 1 : y + 1 + STEP] = a * lam[0] + b * lam[1]
                push_v[1, y + 1 : y + 1 + STEP] = a * lam[1] - b * lam[0]
            else:
                by_shear = (by_a + damp_v[rows] * by_b) * slope_v[rows]
                by_damp = a * by_b
                for h in range(STEP // 4):
                    n = y // 4 + h
                    gout[2 * n, 0] = folded([by_shear[4 * h + q] for q in range(4)])
                    gout[2 * n + 1, 0] = folded([by_damp[4 * h + q] for q in range(4)])
        if t:
            for y in range(0, BY, STEP):
                rows = slice(y, y + STEP)
                push, near = beside_sum(push_v, y)
                lam = lam_v[:, rows]
                lam_v[:, rows] = 1.25 * lam - 6.0 * (push + a_v[rows] * lam) + near

    over_f(lambda p: gout.at[p], in3.at[me_f], 5)
    in3[me_f] = gout[me_f]
    arrived(in3.at[pl.ds(0, freqs - 1)], 5)
    parts = []
    for j in range(group):
        total = in3[j]
        for m in range(1, freqs // group):
            total = total + in3[m * group + j]
        parts.append(total.reshape(subs * K, LANES))
    grads = jnp.concatenate(parts, 0)
    out4[...] = jnp.dot(named, grads, precision=HIGHEST, preferred_element_type=jnp.float32)
    over_z(lambda p: out4.at[pl.ds(p * CAP, CAP)], in4.at[mine2], 6)
    in4[mine2, :] = out4[mine2, :]
    arrived(cnt_in.at[pl.ds(0, (zones - 1) * CAP)], 3)
    uses = jnp.dot(holds, cnt_in[...], precision=HIGHEST, preferred_element_type=jnp.float32)
    scale = 1.0 / (freqs * jnp.maximum(uses, 1.0))
    arrived(in4.at[pl.ds(0, (zones - 1) * CAP)], 6)
    owned = jnp.dot(holds, in4[...], precision=HIGHEST, preferred_element_type=jnp.float32)
    own5[...] = owned * scale
    mine8 = pl.ds(pl.multiple_of(me_f * NB, NB), NB)
    over_f(lambda p: own5, in5.at[mine8], 7)
    in5[mine8, :] = own5[...]
    arrived(in5.at[pl.ds(0, (freqs - 1) * NB)], 7)
    out_ref[...] = in5[...]

    sent(out1.at[pl.ds(0, (zones - 1) * CAP)], 0)
    if group > 1:
        sent(meas_v.at[pl.ds(0, group - 1)], 1)
        sent(wave_v.at[pl.ds(0, group - 1)], 2)
    sent(cnt_out.at[pl.ds(0, (zones - 1) * CAP)], 3)
    sent(in2.at[pl.ds(0, freqs - 1)], 4)
    sent(gout.at[pl.ds(0, freqs - 1)], 5)
    sent(out4.at[pl.ds(0, (zones - 1) * CAP)], 6)
    sent(in5.at[pl.ds(0, (freqs - 1) * NB)], 7)


def update(desc_ref, mod_ref, first_ref, second_ref, fib_ref, new_mod, new_first, new_second):
    lane = lax.broadcasted_iota(jnp.int32, (YH, LANES), 1)
    z = lane % BZ
    for b in range(NB):
        fibre = fib_ref[b * YH : (b + 1) * YH, :]
        square = fibre * fibre
        by_shear = desc_ref[pl.ds(b, YH, stride=2 * NB), :]
        by_damp = desc_ref[pl.ds(NB + b, YH, stride=2 * NB), :]
        by_second = by_shear * square
        for j, descent in enumerate((by_shear - by_second, by_second, by_damp)):
            at = slice((b * 3 + j) * YH, (b * 3 + j + 1) * YH)
            m1 = beta_first * first_ref[at, :] + (1.0 - beta_first) * descent
            m2 = beta_second * second_ref[at, :] + (1.0 - beta_second) * descent * descent
            stepped = mod_ref[at, :] - learn_rate * m1 / (jnp.sqrt(m2) + adam_eps)
            lower = jnp.where(z > 0, pltpu.roll(stepped, 1, 1), stepped)
            upper = jnp.where(z < BZ - 1, pltpu.roll(stepped, LANES - 1, 1), stepped)
            new_first[at, :] = m1
            new_second[at, :] = m2
            new_mod[at, :] = stepped + smooth_rate * square * (0.5 * (lower + upper) - stepped)


def on_device(
    zones, freqs, modulus, first_moment, second_moment, fiber, measured, wave_sq, send_list, brick_list
):
    group = GROUP
    subs = SUBZ // group
    slots = zones * CAP
    mod = modulus.reshape(NB * 3 * YH, LANES)
    m1 = first_moment.reshape(NB * 3 * YH, LANES)
    m2 = second_moment.reshape(NB * 3 * YH, LANES)
    fib = fiber.reshape(NB * YH, LANES)
    meas = measured.reshape(SUBZ, 2, K, YH, LANES).transpose(0, 1, 3, 2, 4)
    f32 = jnp.float32
    vmem = pltpu.VMEM
    any_spec = pl.BlockSpec(memory_space=pl.ANY)
    smem_spec = pl.BlockSpec(memory_space=pltpu.SMEM)
    vmem_spec = pl.BlockSpec(memory_space=vmem)
    plane_shape = (2, YH, K, LANES)
    descent = pl.pallas_call(
        functools.partial(exchange, zones, freqs, group),
        out_shape=jax.ShapeDtypeStruct((freqs * NB, LANES), f32),
        in_specs=[any_spec, any_spec, any_spec, smem_spec, smem_spec, smem_spec],
        out_specs=vmem_spec,
        scratch_shapes=[
            vmem((NB * 3 * YH, LANES), f32),
            vmem((NB * YH, LANES), f32),
            vmem((NB, LANES), f32),
            vmem((slots, LANES), f32),
            vmem((slots, LANES), f32),
            vmem((slots, LANES), f32),
            vmem((slots, LANES), f32),
            vmem((SUBZ, K, LANES), f32),
            vmem((freqs, subs, K, LANES), f32),
            vmem((group, subs) + plane_shape, f32),
            vmem((group, 8, LANES), f32),
            vmem((SWEEPS, 2, BY + 2, K, LANES), f32),
            vmem((SWEEPS, 2, BY, K, LANES), f32),
            vmem((BY, K, LANES), f32),
            vmem((BY, K, LANES), f32),
            vmem((BY, K, LANES), f32),
            vmem((BY, K, LANES), f32),
            vmem((2, BY, K, LANES), f32),
            vmem((2, BY + 2, K, LANES), f32),
            vmem((BY, K, LANES), f32),
            vmem((BY, K, LANES), f32),
            vmem((freqs, subs, K, LANES), f32),
            vmem((freqs, subs, K, LANES), f32),
            vmem((slots, LANES), f32),
            vmem((slots, LANES), f32),
            vmem((NB, LANES), f32),
            vmem((freqs * NB, LANES), f32),
            pltpu.SemaphoreType.DMA((3,)),
            pltpu.SemaphoreType.DMA((8,)),
            pltpu.SemaphoreType.DMA((8,)),
        ],
        compiler_params=pltpu.CompilerParams(
            collective_id=0, has_side_effects=True, vmem_limit_bytes=60 * 2**20
        ),
    )(mod, fib, meas, wave_sq, send_list.transpose(0, 2, 1), brick_list)
    made = jax.ShapeDtypeStruct((NB * 3 * YH, LANES), f32)
    outs = pl.pallas_call(
        update,
        out_shape=(made, made, made),
        in_specs=[vmem_spec] * 5,
        out_specs=(vmem_spec,) * 3,
    )(descent, mod, m1, m2, fib)
    return tuple(o.reshape(modulus.shape) for o in outs)


def solution(mesh):
    placed = (
        P("zone", None, None, None),
        P("zone", None, None, None),
        P("zone", None, None, None),
        P("zone", None, None),
        P("freq", "zone", None, None, None),
        P("freq"),
        P("zone", None, None),
        P("zone", None),
    )
    return jax.shard_map(
        functools.partial(on_device, mesh.shape["zone"], mesh.shape["freq"]),
        mesh=mesh,
        in_specs=placed,
        out_specs=(P("zone", None, None, None),) * 3,
        check_vma=False,
    )
```

```python
import functools

import jax
import jax.numpy as jnp
from jax import lax
from jax.experimental import pallas as pl
from jax.experimental.pallas import tpu as pltpu
from jax.sharding import PartitionSpec as P

BZ = 32
K = 8
NB = 8
SUBZ = 4
CAP = 2
YH = 8
LANES = 128
SWEEPS = 6
BY = 32
STEP = 8
GROUP = 4

relax_rate = 0.25
learn_rate = 0.1
beta_first = 0.9
beta_second = 0.99
smooth_rate = 0.5
adam_eps = 1e-08

MESH = pl.DeviceIdType.MESH


def picked(which, x):
    high = x.astype(jnp.bfloat16)
    rest = x - high.astype(jnp.float32)
    middle = rest.astype(jnp.bfloat16)
    low = (rest - middle.astype(jnp.float32)).astype(jnp.bfloat16)
    which = which.astype(jnp.bfloat16)
    return jnp.dot(
        jnp.concatenate([which, which, which], 1),
        jnp.concatenate([high, middle, low], 0),
        preferred_element_type=jnp.float32,
    )


def quarters(shape=(K, LANES)):
    lane = lax.broadcasted_iota(jnp.int32, shape, len(shape) - 1)
    return lane < 2 * BZ, lane % (2 * BZ) < BZ


def turn(x, n):
    return pltpu.roll(x, n * BZ, 1)


def transposed(x):
    low, even = quarters()
    n0 = jnp.where(low, x[0], turn(x[2], 2))
    n1 = jnp.where(low, x[1], turn(x[3], 2))
    n2 = jnp.where(low, turn(x[0], 2), x[2])
    n3 = jnp.where(low, turn(x[1], 2), x[3])
    return (
        jnp.where(even, n0, turn(n1, 1)),
        jnp.where(even, turn(n0, 3), n1),
        jnp.where(even, n2, turn(n3, 1)),
        jnp.where(even, turn(n2, 3), n3),
    )


def spread(x):
    low, even = quarters()
    r = (x, turn(x, 1), turn(x, 2), turn(x, 3))
    return tuple(
        jnp.where(
            low,
            jnp.where(even, r[(-q) % 4], r[(1 - q) % 4]),
            jnp.where(even, r[(2 - q) % 4], r[(3 - q) % 4]),
        )
        for q in range(4)
    )


def folded(x):
    low, even = quarters()
    p0 = jnp.where(low, x[0], x[2]) + turn(jnp.where(low, x[2], x[0]), 2)
    p1 = jnp.where(low, x[1], x[3]) + turn(jnp.where(low, x[3], x[1]), 2)
    rest = jnp.where(even, p1, p0)
    return jnp.where(even, p0, p1) + jnp.where(even, turn(rest, 3), turn(rest, 1))


def beside_sum(ref, y):
    x = ref[:, y + 1 : y + 1 + STEP]
    lane = lax.broadcasted_iota(jnp.int32, x.shape, 3)
    sub = lax.broadcasted_iota(jnp.int32, x.shape, 2)
    z = lane % BZ
    total = ref[:, y : y + STEP] + ref[:, y + 2 : y + 2 + STEP]
    total += jnp.where(z > 0, pltpu.roll(x, 1, 3), 0.0)
    total += jnp.where(z < BZ - 1, pltpu.roll(x, LANES - 1, 3), 0.0)
    total += jnp.where(sub > 0, pltpu.roll(x, 1, 2), 0.0)
    return x, total + jnp.where(sub < K - 1, pltpu.roll(x, K - 1, 2), 0.0)


def exchange(
    zones,
    freqs,
    group,
    mod_hbm,
    fib_hbm,
    meas_hbm,
    wave_hbm,
    send_hbm,
    brick_hbm,
    out_ref,
    wave_ref,
    send_ref,
    brick_ref,
    mod_v,
    fib_v,
    val_v,
    out1,
    in1,
    cnt_out,
    cnt_in,
    names_v,
    ent,
    in2,
    meas_v,
    wave_v,
    field_v,
    sten_v,
    a_v,
    b_v,
    damp_v,
    slope_v,
    lam_v,
    push_v,
    by_a_v,
    by_b_v,
    gout,
    in3,
    out4,
    in4,
    own5,
    local_sem,
    send_sem,
    recv_sem,
):
    subs = SUBZ // group
    slots = zones * CAP
    heights = zones // 2
    me_zone = lax.axis_index("zone")
    me_z = lax.div(me_zone, 2)
    me_x = lax.rem(me_zone, 2)
    me_f = lax.axis_index("freq")
    me_t = me_x * freqs + me_f
    level = 2 * freqs
    block = 2 * CAP
    plane = lax.rem(me_f, 2)
    row = lax.div(me_f, 2)
    member = lax.rem(me_f, group)
    base = me_f - member

    load_mod = pltpu.make_async_copy(mod_hbm, mod_v, local_sem.at[0])
    load_fib = pltpu.make_async_copy(fib_hbm, fib_v, local_sem.at[1])
    load_meas = pltpu.make_async_copy(
        meas_hbm.at[pl.ds(member * subs, subs)], meas_v.at[member], local_sem.at[2]
    )
    barrier = pltpu.get_barrier_semaphore()

    def far_first(me, i, n):
        k = lax.div(i, 2)
        return lax.rem(me + n + n // 2 + jnp.where(lax.rem(i, 2) == 0, k, -k), n)

    def at_height(z):
        return (z * 2 + me_x, me_f)

    def at_place(t):
        return (me_z * 2 + lax.div(t, freqs), lax.rem(t, freqs))

    def greet_z(i, c):
        peer = at_height(far_first(me_z, i, heights))
        pl.semaphore_signal(barrier, inc=1, device_id=peer, device_id_type=MESH)
        return c

    def greet_near(i, c):
        peer = at_place(far_first(me_t, i, level))
        pl.semaphore_signal(barrier, inc=1, device_id=peer, device_id_type=MESH)
        return c

    lax.fori_loop(1, heights, greet_z, 0)
    lax.fori_loop(1, level, greet_near, 0)
    load_send = pltpu.make_async_copy(send_hbm, send_ref, local_sem.at[3])
    load_brick = pltpu.make_async_copy(brick_hbm, brick_ref, local_sem.at[4])
    load_wave = pltpu.make_async_copy(wave_hbm, wave_ref, local_sem.at[5])
    load_send.start()
    load_mod.start()
    load_fib.start()
    load_brick.start()
    load_wave.start()
    load_meas.start()

    load_mod.wait()
    load_fib.wait()
    first = mod_v[pl.ds(row, NB, stride=3 * YH), :]
    second = mod_v[pl.ds(YH + row, NB, stride=3 * YH), :]
    damp = mod_v[pl.ds(2 * YH + row, NB, stride=3 * YH), :]
    fibre = fib_v[pl.ds(row, NB, stride=YH), :]
    shear = first + (second - first) * fibre * fibre
    val_v[...] = jnp.where(plane == 0, shear, damp)
    load_send.wait()
    for d in range(zones):
        for c in range(CAP):
            pick = jnp.maximum(send_ref[0, c, d], 0)
            out1[d * CAP + c : d * CAP + c + 1, :] = val_v[pl.ds(pick, 1), :]

    pl.semaphore_wait(barrier, heights + level - 2)

    def send_all(me, count, device, src, dst, n):
        def body(i, c):
            peer = far_first(me, i, count)
            pltpu.make_async_remote_copy(
                src_ref=src(peer),
                dst_ref=dst,
                send_sem=send_sem.at[n],
                recv_sem=recv_sem.at[n],
                device_id=device(peer),
                device_id_type=MESH,
            ).start()
            return c

        lax.fori_loop(1, count, body, 0)

    def over_z(src, dst, n):
        send_all(me_z, heights, at_height, src, dst, n)

    def over_near(src, dst, n):
        send_all(me_t, level, at_place, src, dst, n)

    def over_f(src, dst, n):
        send_all(me_f, freqs, lambda f: (me_zone, f), src, dst, n)

    def arrived(ref, n):
        pltpu.make_async_copy(ref, ref, recv_sem.at[n]).wait()

    def sent(ref, n):
        pltpu.make_async_copy(ref, ref, send_sem.at[n]).wait()

    mine4 = pl.ds(pl.multiple_of(me_z * block, block), block)
    others4 = pl.ds(0, (heights - 1) * block)

    def block_of(ref):
        return lambda z: ref.at[pl.ds(pl.multiple_of(z * block, block), block)]

    over_z(block_of(out1), in1.at[mine4], 0)
    in1[mine4, :] = out1[mine4, :]

    load_wave.wait()
    wave_v[member] = jnp.full((8, LANES), wave_ref[0], jnp.float32)

    def share(i, c):
        j = lax.rem(member + i, group)
        pltpu.make_async_remote_copy(
            src_ref=meas_hbm.at[pl.ds(j * subs, subs)],
            dst_ref=meas_v.at[member],
            send_sem=send_sem.at[1],
            recv_sem=recv_sem.at[1],
            device_id=(me_zone, base + j),
            device_id_type=MESH,
        ).start()
        pltpu.make_async_remote_copy(
            src_ref=wave_v.at[member],
            dst_ref=wave_v.at[member],
            send_sem=send_sem.at[2],
            recv_sem=recv_sem.at[2],
            device_id=(me_zone, base + j),
            device_id_type=MESH,
        ).start()
        return c

    if group > 1:
        lax.fori_loop(1, group, share, 0)

    entries = SUBZ * K
    load_brick.wait()
    lane = lax.broadcasted_iota(jnp.int32, (8, LANES), 1)
    names = jnp.full((8, LANES), -1, jnp.int32)
    for e in range(entries):
        names = jnp.where(lane == e, brick_ref[e // K, e % K], names)
    names_v[me_x] = names
    swap = pltpu.make_async_remote_copy(
        src_ref=names_v.at[me_x],
        dst_ref=names_v.at[me_x],
        send_sem=send_sem.at[8],
        recv_sem=recv_sem.at[8],
        device_id=(me_z * 2 + 1 - me_x, me_f),
        device_id_type=MESH,
    )
    swap.start()
    swap.wait_recv()
    both = jnp.where(lane < entries, names_v[0], pltpu.roll(names_v[1], entries, 1))[:1]
    half = lane[:1] // entries
    slot = (both // 4) * 4 + half * CAP + both % 2
    ours = (both // 2) % 2 == me_x
    slot = jnp.where((half < 2) & ours, slot, -1)
    named = (lax.broadcasted_iota(jnp.int32, (slots, LANES), 0) == slot).astype(jnp.float32)
    namers = jnp.transpose(named)[: 2 * entries]
    cnt_out[...] = jnp.broadcast_to(jnp.sum(named, 1, keepdims=True), (slots, LANES))
    over_z(block_of(cnt_out), cnt_in.at[mine4], 3)
    cnt_in[mine4, :] = cnt_out[mine4, :]
    named = named[:, : 2 * entries]

    arrived(in1.at[others4], 0)
    ent[...] = picked(namers, in1[...]).reshape(2 * SUBZ, K, LANES)
    over_near(
        lambda t: ent.at[lax.div(t, freqs) * SUBZ + lax.rem(t, group)],
        in2.at[me_t],
        4,
    )
    in2[me_t] = ent[me_x * SUBZ + member]

    load_meas.wait()
    if group > 1:
        arrived(meas_v.at[pl.ds(0, group - 1)], 1)
        arrived(wave_v.at[pl.ds(0, group - 1)], 2)

    for t in range(SWEEPS):
        field_v[t, :, 0] = jnp.zeros((2, K, LANES), jnp.float32)
        field_v[t, :, BY + 1] = jnp.zeros((2, K, LANES), jnp.float32)
    push_v[:, 0] = jnp.zeros((2, K, LANES), jnp.float32)
    push_v[:, BY + 1] = jnp.zeros((2, K, LANES), jnp.float32)
    for p in range(2):
        for y in range(YH):
            for q, tile in enumerate(transposed([meas_v[g, 0, p, y] for g in range(group)])):
                field_v[0, p, 1 + 4 * y + q] = tile
    low, even = quarters()
    wave = jnp.where(
        low,
        jnp.where(even, wave_v[0], wave_v[1]),
        jnp.where(even, wave_v[2], wave_v[3]),
    )
    for y in range(0, BY, STEP):
        x, near = beside_sum(field_v.at[0], y)
        sten_v[0, :, y : y + STEP] = near - 6.0 * x

    lane_s = lax.broadcasted_iota(jnp.int32, (1, slots), 1)
    held = jnp.zeros((1, slots), jnp.int32)
    for d in range(zones):
        for c in range(CAP):
            held = jnp.where(lane_s == d * CAP + c, send_ref[0, c, d], held)
    holds = (lax.broadcasted_iota(jnp.int32, (NB, slots), 0) == held).astype(jnp.float32)

    arrived(in2.at[pl.ds(0, level - 1)], 4)

    for y in range(YH):
        shears = spread(in2[2 * y] + in2[freqs + 2 * y])
        damps = spread(in2[2 * y + 1] + in2[freqs + 2 * y + 1])
        for q, (shear, damp) in enumerate(zip(shears, damps)):
            inv = 1.0 / (6.0 * shear + wave)
            a = relax_rate * shear * inv
            a_v[4 * y + q] = a
            b_v[4 * y + q] = a * damp
            damp_v[4 * y + q] = damp
            slope_v[4 * y + q] = relax_rate * wave * inv * inv

    for t in range(SWEEPS):
        for y in range(0, BY, STEP):
            rows = slice(y, y + STEP)
            if t:
                x, near = beside_sum(field_v.at[t], y)
                six = 6.0 * x
                w = near - six
                sten_v[t, :, rows] = w
            else:
                x = field_v[0, :, y + 1 : y + 1 + STEP]
                six = 6.0 * x
                w = sten_v[0, :, rows]
            v = w - six
            a, b = a_v[rows], b_v[rows]
            real = 1.25 * x[0] + (a * v[0] - b * w[1])
            imag = 1.25 * x[1] + (a * v[1] + b * w[0])
            if t < SWEEPS - 1:
                field_v[t + 1, 0, y + 1 : y + 1 + STEP] = real
                field_v[t + 1, 1, y + 1 : y + 1 + STEP] = imag
            else:
                lam_v[0, rows] = 2.0 * (real - field_v[0, 0, y + 1 : y + 1 + STEP])
                lam_v[1, rows] = 2.0 * (imag - field_v[0, 1, y + 1 : y + 1 + STEP])
    for t in reversed(range(SWEEPS)):
        for y in range(0, BY, STEP):
            rows = slice(y, y + STEP)
            lam = lam_v[:, rows]
            w = sten_v[t, :, rows]
            v = w - 6.0 * field_v[t, :, y + 1 : y + 1 + STEP]
            by_a = lam[0] * v[0] + lam[1] * v[1]
            by_b = lam[1] * w[0] - lam[0] * w[1]
            if t < SWEEPS - 1:
                by_a += by_a_v[rows]
                by_b += by_b_v[rows]
            a, b = a_v[rows], b_v[rows]
            if t:
                by_a_v[rows] = by_a
                by_b_v[rows] = by_b
                push_v[0, y + 1 : y + 1 + STEP] = a * lam[0] + b * lam[1]
                push_v[1, y + 1 : y + 1 + STEP] = a * lam[1] - b * lam[0]
            else:
                by_shear = (by_a + damp_v[rows] * by_b) * slope_v[rows]
                by_damp = a * by_b
                for h in range(STEP // 4):
                    n = y // 4 + h
                    gout[2 * n] = folded([by_shear[4 * h + q] for q in range(4)])
                    gout[2 * n + 1] = folded([by_damp[4 * h + q] for q in range(4)])
        if t:
            for y in range(0, BY, STEP):
                rows = slice(y, y + STEP)
                push, near = beside_sum(push_v, y)
                lam = lam_v[:, rows]
                lam_v[:, rows] = 1.25 * lam - 6.0 * (push + a_v[rows] * lam) + near

    over_near(lambda t: gout.at[lax.rem(t, freqs)], in3.at[me_t], 5)
    in3[me_t] = gout[me_f]
    arrived(in3.at[pl.ds(0, level - 1)], 5)
    parts = []
    for h in range(2):
        for j in range(group):
            total = in3[h * freqs + j]
            for m in range(1, freqs // group):
                total = total + in3[h * freqs + m * group + j]
            parts.append(total)
    out4[...] = picked(named, jnp.concatenate(parts, 0))
    over_z(block_of(out4), in4.at[mine4], 6)
    in4[mine4, :] = out4[mine4, :]
    arrived(cnt_in.at[others4], 3)
    uses = picked(holds, cnt_in[...])
    scale = 1.0 / (freqs * jnp.maximum(uses, 1.0))
    arrived(in4.at[others4], 6)
    owned = picked(holds, in4[...])
    own5[...] = owned * scale
    mine8 = pl.ds(pl.multiple_of(me_f * NB, NB), NB)
    over_f(lambda p: own5, out_ref.at[mine8], 7)
    keep = pltpu.make_async_copy(own5, out_ref.at[mine8], local_sem.at[0])
    keep.start()
    arrived(out_ref.at[pl.ds(0, (freqs - 1) * NB)], 7)
    keep.wait()

    sent(out1.at[others4], 0)
    if group > 1:
        sent(meas_v.at[pl.ds(0, group - 1)], 1)
        sent(wave_v.at[pl.ds(0, group - 1)], 2)
    sent(cnt_out.at[others4], 3)
    swap.wait_send()
    sent(in2.at[pl.ds(0, level - 1)], 4)
    sent(in3.at[pl.ds(0, level - 1)], 5)
    sent(out4.at[others4], 6)
    sent(out_ref.at[pl.ds(0, (freqs - 1) * NB)], 7)


def update(desc_ref, mod_ref, first_ref, second_ref, fib_ref, new_mod, new_first, new_second):
    lane = lax.broadcasted_iota(jnp.int32, (YH, LANES), 1)
    z = lane % BZ
    for b in range(NB):
        fibre = fib_ref[b * YH : (b + 1) * YH, :]
        square = fibre * fibre
        by_shear = desc_ref[pl.ds(b, YH, stride=2 * NB), :]
        by_damp = desc_ref[pl.ds(NB + b, YH, stride=2 * NB), :]
        by_second = by_shear * square
        for j, descent in enumerate((by_shear - by_second, by_second, by_damp)):
            at = slice((b * 3 + j) * YH, (b * 3 + j + 1) * YH)
            m1 = beta_first * first_ref[at, :] + (1.0 - beta_first) * descent
            m2 = beta_second * second_ref[at, :] + (1.0 - beta_second) * descent * descent
            stepped = mod_ref[at, :] - learn_rate * m1 / (jnp.sqrt(m2) + adam_eps)
            lower = jnp.where(z > 0, pltpu.roll(stepped, 1, 1), stepped)
            upper = jnp.where(z < BZ - 1, pltpu.roll(stepped, LANES - 1, 1), stepped)
            new_first[at, :] = m1
            new_second[at, :] = m2
            new_mod[at, :] = stepped + smooth_rate * square * (0.5 * (lower + upper) - stepped)


def on_device(
    zones, freqs, modulus, first_moment, second_moment, fiber, measured, wave_sq, send_list, brick_list
):
    group = GROUP
    subs = SUBZ // group
    slots = zones * CAP
    mod = modulus.reshape(NB * 3 * YH, LANES)
    m1 = first_moment.reshape(NB * 3 * YH, LANES)
    m2 = second_moment.reshape(NB * 3 * YH, LANES)
    fib = fiber.reshape(NB * YH, LANES)
    meas = measured.reshape(SUBZ, 2, K, YH, LANES).transpose(0, 1, 3, 2, 4)
    f32 = jnp.float32
    vmem = pltpu.VMEM
    any_spec = pl.BlockSpec(memory_space=pl.ANY)
    vmem_spec = pl.BlockSpec(memory_space=vmem)
    plane_shape = (2, YH, K, LANES)
    descent = pl.pallas_call(
        functools.partial(exchange, zones, freqs, group),
        out_shape=jax.ShapeDtypeStruct((freqs * NB, LANES), f32),
        in_specs=[any_spec, any_spec, any_spec, any_spec, any_spec, any_spec],
        out_specs=any_spec,
        scratch_shapes=[
            pltpu.SMEM((1,), f32),
            pltpu.SMEM((1, CAP, zones), jnp.int32),
            pltpu.SMEM((SUBZ, K), jnp.int32),
            vmem((NB * 3 * YH, LANES), f32),
            vmem((NB * YH, LANES), f32),
            vmem((NB, LANES), f32),
            vmem((slots, LANES), f32),
            vmem((slots, LANES), f32),
            vmem((slots, LANES), f32),
            vmem((slots, LANES), f32),
            vmem((2, 8, LANES), jnp.int32),
            vmem((2 * SUBZ, K, LANES), f32),
            vmem((2 * freqs, K, LANES), f32),
            vmem((group, subs) + plane_shape, f32),
            vmem((group, 8, LANES), f32),
            vmem((SWEEPS, 2, BY + 2, K, LANES), f32),
            vmem((SWEEPS, 2, BY, K, LANES), f32),
            vmem((BY, K, LANES), f32),
            vmem((BY, K, LANES), f32),
            vmem((BY, K, LANES), f32),
            vmem((BY, K, LANES), f32),
            vmem((2, BY, K, LANES), f32),
            vmem((2, BY + 2, K, LANES), f32),
            vmem((BY, K, LANES), f32),
            vmem((BY, K, LANES), f32),
            vmem((freqs, K, LANES), f32),
            vmem((2 * freqs, K, LANES), f32),
            vmem((slots, LANES), f32),
            vmem((slots, LANES), f32),
            vmem((NB, LANES), f32),
            pltpu.SemaphoreType.DMA((6,)),
            pltpu.SemaphoreType.DMA((9,)),
            pltpu.SemaphoreType.DMA((9,)),
        ],
        compiler_params=pltpu.CompilerParams(
            collective_id=0, has_side_effects=True, vmem_limit_bytes=60 * 2**20
        ),
    )(mod, fib, meas, wave_sq, send_list.transpose(0, 2, 1), brick_list)
    made = jax.ShapeDtypeStruct((NB * 3 * YH, LANES), f32)
    outs = pl.pallas_call(
        update,
        out_shape=(made, made, made),
        in_specs=[vmem_spec] * 5,
        out_specs=(vmem_spec,) * 3,
    )(descent, mod, m1, m2, fib)
    return tuple(o.reshape(modulus.shape) for o in outs)


def solution(mesh):
    placed = (
        P("zone", None, None, None),
        P("zone", None, None, None),
        P("zone", None, None, None),
        P("zone", None, None),
        P("freq", "zone", None, None, None),
        P("freq"),
        P("zone", None, None),
        P("zone", None),
    )
    return jax.shard_map(
        functools.partial(on_device, mesh.shape["zone"], mesh.shape["freq"]),
        mesh=mesh,
        in_specs=placed,
        out_specs=(P("zone", None, None, None),) * 3,
        check_vma=False,
    )
```

```python
import functools

import jax
import jax.numpy as jnp
from jax import lax
from jax.experimental import pallas as pl
from jax.experimental.pallas import tpu as pltpu
from jax.sharding import PartitionSpec as P

BZ = 32
K = 8
NB = 8
SUBZ = 4
CAP = 2
YH = 8
LANES = 128
SWEEPS = 6
BY = 32
STEP = 16
GROUP = 4

relax_rate = 0.25
learn_rate = 0.1
beta_first = 0.9
beta_second = 0.99
smooth_rate = 0.5
adam_eps = 1e-08

MESH = pl.DeviceIdType.MESH


def picked(which, x):
    high = x.astype(jnp.bfloat16)
    rest = x - high.astype(jnp.float32)
    middle = rest.astype(jnp.bfloat16)
    low = (rest - middle.astype(jnp.float32)).astype(jnp.bfloat16)
    which = which.astype(jnp.bfloat16)
    return jnp.dot(
        jnp.concatenate([which, which, which], 1),
        jnp.concatenate([high, middle, low], 0),
        preferred_element_type=jnp.float32,
    )


def quarters(shape=(K, LANES)):
    lane = lax.broadcasted_iota(jnp.int32, shape, len(shape) - 1)
    return lane < 2 * BZ, lane % (2 * BZ) < BZ


def turn(x, n):
    return pltpu.roll(x, n * BZ, 1)


def transposed(x):
    low, even = quarters()
    n0 = jnp.where(low, x[0], turn(x[2], 2))
    n1 = jnp.where(low, x[1], turn(x[3], 2))
    n2 = jnp.where(low, turn(x[0], 2), x[2])
    n3 = jnp.where(low, turn(x[1], 2), x[3])
    return (
        jnp.where(even, n0, turn(n1, 1)),
        jnp.where(even, turn(n0, 3), n1),
        jnp.where(even, n2, turn(n3, 1)),
        jnp.where(even, turn(n2, 3), n3),
    )


def spread(x):
    low, even = quarters()
    r = (x, turn(x, 1), turn(x, 2), turn(x, 3))
    return tuple(
        jnp.where(
            low,
            jnp.where(even, r[(-q) % 4], r[(1 - q) % 4]),
            jnp.where(even, r[(2 - q) % 4], r[(3 - q) % 4]),
        )
        for q in range(4)
    )


def folded(x):
    low, even = quarters()
    p0 = jnp.where(low, x[0], x[2]) + turn(jnp.where(low, x[2], x[0]), 2)
    p1 = jnp.where(low, x[1], x[3]) + turn(jnp.where(low, x[3], x[1]), 2)
    rest = jnp.where(even, p1, p0)
    return jnp.where(even, p0, p1) + jnp.where(even, turn(rest, 3), turn(rest, 1))


def beside_sum(ref, y):
    x = ref[:, y + 1 : y + 1 + STEP]
    lane = lax.broadcasted_iota(jnp.int32, x.shape, 3)
    sub = lax.broadcasted_iota(jnp.int32, x.shape, 2)
    z = lane % BZ
    total = ref[:, y : y + STEP] + ref[:, y + 2 : y + 2 + STEP]
    total += jnp.where(z > 0, pltpu.roll(x, 1, 3), 0.0)
    total += jnp.where(z < BZ - 1, pltpu.roll(x, LANES - 1, 3), 0.0)
    total += jnp.where(sub > 0, pltpu.roll(x, 1, 2), 0.0)
    return x, total + jnp.where(sub < K - 1, pltpu.roll(x, K - 1, 2), 0.0)


def exchange(
    zones,
    freqs,
    group,
    mod_hbm,
    fib_hbm,
    meas_hbm,
    wave_hbm,
    send_hbm,
    brick_hbm,
    out_ref,
    wave_ref,
    send_ref,
    brick_ref,
    mod_v,
    fib_v,
    val_v,
    out1,
    in1,
    cnt_out,
    cnt_in,
    names_v,
    ent,
    in2,
    meas_v,
    wave_v,
    field_v,
    sten_v,
    a_v,
    b_v,
    damp_v,
    slope_v,
    lam_v,
    push_v,
    by_a_v,
    by_b_v,
    gout,
    in3,
    out4,
    in4,
    own5,
    local_sem,
    send_sem,
    recv_sem,
):
    subs = SUBZ // group
    slots = zones * CAP
    heights = zones // 2
    me_zone = lax.axis_index("zone")
    me_z = lax.div(me_zone, 2)
    me_x = lax.rem(me_zone, 2)
    me_f = lax.axis_index("freq")
    me_t = me_x * freqs + me_f
    level = 2 * freqs
    block = 2 * CAP
    plane = lax.rem(me_f, 2)
    row = lax.div(me_f, 2)
    member = lax.rem(me_f, group)
    base = me_f - member

    load_mod = pltpu.make_async_copy(mod_hbm, mod_v, local_sem.at[0])
    load_fib = pltpu.make_async_copy(fib_hbm, fib_v, local_sem.at[1])
    load_meas = pltpu.make_async_copy(
        meas_hbm.at[pl.ds(member * subs, subs)], meas_v.at[member], local_sem.at[2]
    )
    barrier = pltpu.get_barrier_semaphore()

    def far_first(me, i, n):
        k = lax.div(i, 2)
        return lax.rem(me + n + n // 2 + jnp.where(lax.rem(i, 2) == 0, k, -k), n)

    def at_height(z):
        return (z * 2 + me_x, me_f)

    def at_place(t):
        return (me_z * 2 + lax.div(t, freqs), lax.rem(t, freqs))

    def greet_z(i, c):
        peer = at_height(far_first(me_z, i, heights))
        pl.semaphore_signal(barrier, inc=1, device_id=peer, device_id_type=MESH)
        return c

    def greet_near(i, c):
        peer = at_place(far_first(me_t, i, level))
        pl.semaphore_signal(barrier, inc=1, device_id=peer, device_id_type=MESH)
        return c

    lax.fori_loop(1, heights, greet_z, 0)
    lax.fori_loop(1, level, greet_near, 0)
    load_send = pltpu.make_async_copy(send_hbm, send_ref, local_sem.at[3])
    load_brick = pltpu.make_async_copy(brick_hbm, brick_ref, local_sem.at[4])
    load_wave = pltpu.make_async_copy(wave_hbm, wave_ref, local_sem.at[5])
    load_send.start()
    load_mod.start()
    load_fib.start()
    load_brick.start()
    load_wave.start()
    load_meas.start()

    load_mod.wait()
    load_fib.wait()
    first = mod_v[pl.ds(row, NB, stride=3 * YH), :]
    second = mod_v[pl.ds(YH + row, NB, stride=3 * YH), :]
    damp = mod_v[pl.ds(2 * YH + row, NB, stride=3 * YH), :]
    fibre = fib_v[pl.ds(row, NB, stride=YH), :]
    shear = first + (second - first) * fibre * fibre
    val_v[...] = jnp.where(plane == 0, shear, damp)
    load_send.wait()
    for d in range(zones):
        for c in range(CAP):
            pick = jnp.maximum(send_ref[0, c, d], 0)
            out1[d * CAP + c : d * CAP + c + 1, :] = val_v[pl.ds(pick, 1), :]

    pl.semaphore_wait(barrier, heights + level - 2)

    def send_all(me, count, device, src, dst, n):
        def body(i, c):
            peer = far_first(me, i, count)
            pltpu.make_async_remote_copy(
                src_ref=src(peer),
                dst_ref=dst,
                send_sem=send_sem.at[n],
                recv_sem=recv_sem.at[n],
                device_id=device(peer),
                device_id_type=MESH,
            ).start()
            return c

        lax.fori_loop(1, count, body, 0)

    def over_z(src, dst, n):
        send_all(me_z, heights, at_height, src, dst, n)

    def over_near(src, dst, n):
        send_all(me_t, level, at_place, src, dst, n)

    def over_f(src, dst, n):
        send_all(me_f, freqs, lambda f: (me_zone, f), src, dst, n)

    def arrived(ref, n):
        pltpu.make_async_copy(ref, ref, recv_sem.at[n]).wait()

    def sent(ref, n):
        pltpu.make_async_copy(ref, ref, send_sem.at[n]).wait()

    mine4 = pl.ds(pl.multiple_of(me_z * block, block), block)
    others4 = pl.ds(0, (heights - 1) * block)

    def block_of(ref):
        return lambda z: ref.at[pl.ds(pl.multiple_of(z * block, block), block)]

    over_z(block_of(out1), in1.at[mine4], 0)
    in1[mine4, :] = out1[mine4, :]

    load_wave.wait()
    wave_v[member] = jnp.full((8, LANES), wave_ref[0], jnp.float32)

    def share(i, c):
        j = lax.rem(member + i, group)
        pltpu.make_async_remote_copy(
            src_ref=meas_hbm.at[pl.ds(j * subs, subs)],
            dst_ref=meas_v.at[member],
            send_sem=send_sem.at[1],
            recv_sem=recv_sem.at[1],
            device_id=(me_zone, base + j),
            device_id_type=MESH,
        ).start()
        pltpu.make_async_remote_copy(
            src_ref=wave_v.at[member],
            dst_ref=wave_v.at[member],
            send_sem=send_sem.at[2],
            recv_sem=recv_sem.at[2],
            device_id=(me_zone, base + j),
            device_id_type=MESH,
        ).start()
        return c

    if group > 1:
        lax.fori_loop(1, group, share, 0)

    entries = SUBZ * K
    load_brick.wait()
    lane = lax.broadcasted_iota(jnp.int32, (8, LANES), 1)
    names = jnp.full((8, LANES), -1, jnp.int32)
    for e in range(entries):
        names = jnp.where(lane == e, brick_ref[e // K, e % K], names)
    names_v[me_x] = names
    swap = pltpu.make_async_remote_copy(
        src_ref=names_v.at[me_x],
        dst_ref=names_v.at[me_x],
        send_sem=send_sem.at[8],
        recv_sem=recv_sem.at[8],
        device_id=(me_z * 2 + 1 - me_x, me_f),
        device_id_type=MESH,
    )
    swap.start()
    swap.wait_recv()
    both = jnp.where(lane < entries, names_v[0], pltpu.roll(names_v[1], entries, 1))[:1]
    half = lane[:1] // entries
    slot = (both // 4) * 4 + half * CAP + both % 2
    ours = (both // 2) % 2 == me_x
    slot = jnp.where((half < 2) & ours, slot, -1)
    named = (lax.broadcasted_iota(jnp.int32, (slots, LANES), 0) == slot).astype(jnp.float32)
    namers = jnp.transpose(named)[: 2 * entries]
    cnt_out[...] = jnp.broadcast_to(jnp.sum(named, 1, keepdims=True), (slots, LANES))
    over_z(block_of(cnt_out), cnt_in.at[mine4], 3)
    cnt_in[mine4, :] = cnt_out[mine4, :]
    named = named[:, : 2 * entries]

    arrived(in1.at[others4], 0)
    ent[...] = picked(namers, in1[...]).reshape(2 * SUBZ, K, LANES)
    over_near(
        lambda t: ent.at[lax.div(t, freqs) * SUBZ + lax.rem(t, group)],
        in2.at[me_t],
        4,
    )
    in2[me_t] = ent[me_x * SUBZ + member]

    load_meas.wait()
    if group > 1:
        arrived(meas_v.at[pl.ds(0, group - 1)], 1)
        arrived(wave_v.at[pl.ds(0, group - 1)], 2)

    for t in range(SWEEPS):
        field_v[t, :, 0] = jnp.zeros((2, K, LANES), jnp.float32)
        field_v[t, :, BY + 1] = jnp.zeros((2, K, LANES), jnp.float32)
    for n in range(2):
        push_v[n, :, 0] = jnp.zeros((2, K, LANES), jnp.float32)
        push_v[n, :, BY + 1] = jnp.zeros((2, K, LANES), jnp.float32)
    for p in range(2):
        for y in range(YH):
            for q, tile in enumerate(transposed([meas_v[g, 0, p, y] for g in range(group)])):
                field_v[0, p, 1 + 4 * y + q] = tile
    low, even = quarters()
    wave = jnp.where(
        low,
        jnp.where(even, wave_v[0], wave_v[1]),
        jnp.where(even, wave_v[2], wave_v[3]),
    )
    for y in range(0, BY, STEP):
        x, near = beside_sum(field_v.at[0], y)
        sten_v[0, :, y : y + STEP] = near - 6.0 * x

    lane_s = lax.broadcasted_iota(jnp.int32, (1, slots), 1)
    held = jnp.zeros((1, slots), jnp.int32)
    for d in range(zones):
        for c in range(CAP):
            held = jnp.where(lane_s == d * CAP + c, send_ref[0, c, d], held)
    holds = (lax.broadcasted_iota(jnp.int32, (NB, slots), 0) == held).astype(jnp.float32)

    arrived(in2.at[pl.ds(0, level - 1)], 4)

    for y in range(YH):
        shears = spread(in2[2 * y] + in2[freqs + 2 * y])
        damps = spread(in2[2 * y + 1] + in2[freqs + 2 * y + 1])
        for q, (shear, damp) in enumerate(zip(shears, damps)):
            inv = 1.0 / (6.0 * shear + wave)
            a = relax_rate * shear * inv
            a_v[4 * y + q] = a
            b_v[4 * y + q] = a * damp
            damp_v[4 * y + q] = damp
            slope_v[4 * y + q] = relax_rate * wave * inv * inv

    for t in range(SWEEPS):
        for y in range(0, BY, STEP):
            rows = slice(y, y + STEP)
            if t:
                x, near = beside_sum(field_v.at[t], y)
                six = 6.0 * x
                w = near - six
                sten_v[t, :, rows] = w
            else:
                x = field_v[0, :, y + 1 : y + 1 + STEP]
                six = 6.0 * x
                w = sten_v[0, :, rows]
            v = w - six
            a, b = a_v[rows], b_v[rows]
            real = 1.25 * x[0] + (a * v[0] - b * w[1])
            imag = 1.25 * x[1] + (a * v[1] + b * w[0])
            if t < SWEEPS - 1:
                field_v[t + 1, 0, y + 1 : y + 1 + STEP] = real
                field_v[t + 1, 1, y + 1 : y + 1 + STEP] = imag
            else:
                lam_v[0, rows] = 2.0 * (real - field_v[0, 0, y + 1 : y + 1 + STEP])
                lam_v[1, rows] = 2.0 * (imag - field_v[0, 1, y + 1 : y + 1 + STEP])
    for t in reversed(range(SWEEPS)):
        for y in range(0, BY, STEP):
            rows = slice(y, y + STEP)
            inner = slice(y + 1, y + 1 + STEP)
            a, b = a_v[rows], b_v[rows]
            lam = lam_v[:, rows]
            if t < SWEEPS - 1:
                push, near = beside_sum(push_v.at[(t + 1) % 2], y)
                lam = 1.25 * lam - 6.0 * (push + a * lam) + near
                if t:
                    lam_v[:, rows] = lam
            w = sten_v[t, :, rows]
            v = w - 6.0 * field_v[t, :, inner]
            by_a = lam[0] * v[0] + lam[1] * v[1]
            by_b = lam[1] * w[0] - lam[0] * w[1]
            if t < SWEEPS - 1:
                by_a += by_a_v[rows]
                by_b += by_b_v[rows]
            if t:
                by_a_v[rows] = by_a
                by_b_v[rows] = by_b
                push_v[t % 2, 0, inner] = a * lam[0] + b * lam[1]
                push_v[t % 2, 1, inner] = a * lam[1] - b * lam[0]
            else:
                by_shear = (by_a + damp_v[rows] * by_b) * slope_v[rows]
                by_damp = a * by_b
                for h in range(STEP // 4):
                    n = y // 4 + h
                    gout[2 * n] = folded([by_shear[4 * h + q] for q in range(4)])
                    gout[2 * n + 1] = folded([by_damp[4 * h + q] for q in range(4)])

    over_near(lambda t: gout.at[lax.rem(t, freqs)], in3.at[me_t], 5)
    in3[me_t] = gout[me_f]
    arrived(in3.at[pl.ds(0, level - 1)], 5)
    parts = []
    for h in range(2):
        for j in range(group):
            total = in3[h * freqs + j]
            for m in range(1, freqs // group):
                total = total + in3[h * freqs + m * group + j]
            parts.append(total)
    out4[...] = picked(named, jnp.concatenate(parts, 0))
    over_z(block_of(out4), in4.at[mine4], 6)
    in4[mine4, :] = out4[mine4, :]
    arrived(cnt_in.at[others4], 3)
    uses = picked(holds, cnt_in[...])
    scale = 1.0 / (freqs * jnp.maximum(uses, 1.0))
    arrived(in4.at[others4], 6)
    owned = picked(holds, in4[...])
    own5[...] = owned * scale
    mine8 = pl.ds(pl.multiple_of(me_f * NB, NB), NB)
    over_f(lambda p: own5, out_ref.at[mine8], 7)
    keep = pltpu.make_async_copy(own5, out_ref.at[mine8], local_sem.at[0])
    keep.start()
    arrived(out_ref.at[pl.ds(0, (freqs - 1) * NB)], 7)
    keep.wait()

    sent(out1.at[others4], 0)
    if group > 1:
        sent(meas_v.at[pl.ds(0, group - 1)], 1)
        sent(wave_v.at[pl.ds(0, group - 1)], 2)
    sent(cnt_out.at[others4], 3)
    swap.wait_send()
    sent(in2.at[pl.ds(0, level - 1)], 4)
    sent(in3.at[pl.ds(0, level - 1)], 5)
    sent(out4.at[others4], 6)
    sent(out_ref.at[pl.ds(0, (freqs - 1) * NB)], 7)


def update(desc_ref, mod_ref, first_ref, second_ref, fib_ref, new_mod, new_first, new_second):
    lane = lax.broadcasted_iota(jnp.int32, (YH, LANES), 1)
    z = lane % BZ
    for b in range(NB):
        fibre = fib_ref[b * YH : (b + 1) * YH, :]
        square = fibre * fibre
        by_shear = desc_ref[pl.ds(b, YH, stride=2 * NB), :]
        by_damp = desc_ref[pl.ds(NB + b, YH, stride=2 * NB), :]
        by_second = by_shear * square
        for j, descent in enumerate((by_shear - by_second, by_second, by_damp)):
            at = slice((b * 3 + j) * YH, (b * 3 + j + 1) * YH)
            m1 = beta_first * first_ref[at, :] + (1.0 - beta_first) * descent
            m2 = beta_second * second_ref[at, :] + (1.0 - beta_second) * descent * descent
            stepped = mod_ref[at, :] - learn_rate * m1 / (jnp.sqrt(m2) + adam_eps)
            lower = jnp.where(z > 0, pltpu.roll(stepped, 1, 1), stepped)
            upper = jnp.where(z < BZ - 1, pltpu.roll(stepped, LANES - 1, 1), stepped)
            new_first[at, :] = m1
            new_second[at, :] = m2
            new_mod[at, :] = stepped + smooth_rate * square * (0.5 * (lower + upper) - stepped)


def on_device(
    zones, freqs, modulus, first_moment, second_moment, fiber, measured, wave_sq, send_list, brick_list
):
    group = GROUP
    subs = SUBZ // group
    slots = zones * CAP
    mod = modulus.reshape(NB * 3 * YH, LANES)
    m1 = first_moment.reshape(NB * 3 * YH, LANES)
    m2 = second_moment.reshape(NB * 3 * YH, LANES)
    fib = fiber.reshape(NB * YH, LANES)
    meas = measured.reshape(SUBZ, 2, K, YH, LANES).transpose(0, 1, 3, 2, 4)
    f32 = jnp.float32
    vmem = pltpu.VMEM
    any_spec = pl.BlockSpec(memory_space=pl.ANY)
    vmem_spec = pl.BlockSpec(memory_space=vmem)
    plane_shape = (2, YH, K, LANES)
    descent = pl.pallas_call(
        functools.partial(exchange, zones, freqs, group),
        out_shape=jax.ShapeDtypeStruct((freqs * NB, LANES), f32),
        in_specs=[any_spec, any_spec, any_spec, any_spec, any_spec, any_spec],
        out_specs=any_spec,
        scratch_shapes=[
            pltpu.SMEM((1,), f32),
            pltpu.SMEM((1, CAP, zones), jnp.int32),
            pltpu.SMEM((SUBZ, K), jnp.int32),
            vmem((NB * 3 * YH, LANES), f32),
            vmem((NB * YH, LANES), f32),
            vmem((NB, LANES), f32),
            vmem((slots, LANES), f32),
            vmem((slots, LANES), f32),
            vmem((slots, LANES), f32),
            vmem((slots, LANES), f32),
            vmem((2, 8, LANES), jnp.int32),
            vmem((2 * SUBZ, K, LANES), f32),
            vmem((2 * freqs, K, LANES), f32),
            vmem((group, subs) + plane_shape, f32),
            vmem((group, 8, LANES), f32),
            vmem((SWEEPS, 2, BY + 2, K, LANES), f32),
            vmem((SWEEPS, 2, BY, K, LANES), f32),
            vmem((BY, K, LANES), f32),
            vmem((BY, K, LANES), f32),
            vmem((BY, K, LANES), f32),
            vmem((BY, K, LANES), f32),
            vmem((2, BY, K, LANES), f32),
            vmem((2, 2, BY + 2, K, LANES), f32),
            vmem((BY, K, LANES), f32),
            vmem((BY, K, LANES), f32),
            vmem((freqs, K, LANES), f32),
            vmem((2 * freqs, K, LANES), f32),
            vmem((slots, LANES), f32),
            vmem((slots, LANES), f32),
            vmem((NB, LANES), f32),
            pltpu.SemaphoreType.DMA((6,)),
            pltpu.SemaphoreType.DMA((9,)),
            pltpu.SemaphoreType.DMA((9,)),
        ],
        compiler_params=pltpu.CompilerParams(
            collective_id=0, has_side_effects=True, vmem_limit_bytes=60 * 2**20
        ),
    )(mod, fib, meas, wave_sq, send_list.transpose(0, 2, 1), brick_list)
    made = jax.ShapeDtypeStruct((NB * 3 * YH, LANES), f32)
    outs = pl.pallas_call(
        update,
        out_shape=(made, made, made),
        in_specs=[vmem_spec] * 5,
        out_specs=(vmem_spec,) * 3,
    )(descent, mod, m1, m2, fib)
    return tuple(o.reshape(modulus.shape) for o in outs)


def solution(mesh):
    placed = (
        P("zone", None, None, None),
        P("zone", None, None, None),
        P("zone", None, None, None),
        P("zone", None, None),
        P("freq", "zone", None, None, None),
        P("freq"),
        P("zone", None, None),
        P("zone", None),
    )
    return jax.shard_map(
        functools.partial(on_device, mesh.shape["zone"], mesh.shape["freq"]),
        mesh=mesh,
        in_specs=placed,
        out_specs=(P("zone", None, None, None),) * 3,
        check_vma=False,
    )
```
